512 devices in a mesh: outer: 16 (over x, y_lo, core), inner: 32 (over y_hi, z).
Axes of the slice: x: 4, y: 8 (y_hi: 4, y_lo: 2; y = y_hi * 2 + y_lo), z: 8, core: 2. Of those that a mesh axis runs over, the one named last changes fastest.
Arguments:
- queries: bfloat16 [65536, 4096], P(('outer', 'inner'))
- keys: bfloat16 [65536, 512], P(('outer', 'inner'))
- values: bfloat16 [65536, 512], P(('outer', 'inner')), may hold values from -6 to 6
- grad_out: bfloat16 [65536, 4096], P(('outer', 'inner')), may hold values from -6 to 6
- doc_start: int32 [65536], P(('outer', 'inner')), may hold values from 0 to 65535, as said below
Outputs:
- grad_queries: bfloat16 [65536, 4096], P(('outer', 'inner'))
- grad_keys: bfloat16 [65536, 512], P(('outer', 'inner'))
- grad_values: bfloat16 [65536, 512], P(('outer', 'inner'))
The draws below stay inside these ranges and needn't reach their ends.
Inputs may be any that keep to these rules, and one draw needn't show every extreme that they name: doc_start is non-decreasing along the sequence and doc_start[t] <= t; equal values mark one document; every document has 1 to 512 tokens and the first has exactly 512.
All inputs are finite; a program needn't handle non-finite values.
Results may differ from the reference program's by a relative error of at most 0.012.
The reference program's roundings to bfloat16 on the way (of `probs_low` and `dscores`) count: a program that leaves them out, or rounds other values in their place, can miss the bound.
Values may be sent and summed in bfloat16 or wider, within the bound.
No kernel may reach another device: no remote copies, remote signals or barrier semaphores. Data moves between devices by JAX's collectives and lax.ppermute only.
A program may use at most 128 MiB of HBM per device.

```python
import jax
import jax.numpy as jnp
from jax import lax

QUERY_HEADS = 32
KEY_VALUE_HEADS = 4
HEAD_SIZE = 128
TOK_DEV = 128
SPAN = 4
DOC_MOST = 512
PACKED_TOKENS = 65536


def base_keys(key):
    return jax.random.normal(key, (PACKED_TOKENS, KEY_VALUE_HEADS * HEAD_SIZE), jnp.float32)


def draw_keys(key, part):
    shared_window = base_keys(key)
    return shared_window.astype(jnp.bfloat16)


def draw_queries(key, part):
    key = jax.random.fold_in(key, 7)
    fresh = jax.random.normal(key, (PACKED_TOKENS, QUERY_HEADS * HEAD_SIZE), jnp.float32)
    return fresh.astype(jnp.bfloat16)


def draw_doc_start(key, part):
    key = jax.random.fold_in(key, 11)
    lengths = jax.random.randint(key, (PACKED_TOKENS,), 1, DOC_MOST + 1, dtype=jnp.int32)
    lengths = lengths.at[0].set(DOC_MOST)
    ends = jnp.cumsum(lengths)
    starts = ends - lengths
    marks = jnp.zeros((PACKED_TOKENS,), jnp.int32).at[starts].set(1, mode='drop')
    position = jnp.arange(PACKED_TOKENS, dtype=jnp.int32)
    return lax.cummax(jnp.where(marks == 1, position, 0), axis=0)


def block_scale(stream_key, dims, pieces, least, high):
    level = 1.0
    for dim, shards_of in pieces:
        draws = jax.random.uniform(jax.random.fold_in(jax.random.fold_in(stream_key, 6), dim), (shards_of,), jnp.float32, least / len(pieces), high / len(pieces))
        level = level * jnp.repeat(jnp.exp(draws), dims[dim] // shards_of).reshape((-1,) + (1,) * (len(dims) - 1 - dim))
    return level


def noise(rng, shape, scale, limit, shards=(), kind=jnp.bfloat16):
    drawn = scale * jax.random.normal(rng, shape, jnp.float32)
    if shards:
        drawn = drawn * block_scale(rng, shape, shards, -0.22, 0.18)
    return jnp.clip(drawn, -limit, limit).astype(kind)


def setup_inputs(seed: int = 0) -> dict:
    key_list = jax.random.split(jax.random.key(seed), 6)
    return {
        "queries": draw_queries(jax.random.fold_in(key_list[5], 71), 0),
        "keys": draw_keys(jax.random.fold_in(key_list[5], 71), 0),
        "values": noise(key_list[2], (PACKED_TOKENS, KEY_VALUE_HEADS * HEAD_SIZE), 1.0, 6.0, ((0, 512),)),
        "grad_out": noise(key_list[3], (PACKED_TOKENS, QUERY_HEADS * HEAD_SIZE), 1.0, 6.0, ((0, 512),)),
        "doc_start": draw_doc_start(jax.random.fold_in(key_list[5], 71), 0),
    }


def head_group(queries, grad_out, key_window, value_window, visible_mask, group, query_per_key_head, head_dim):
    tok_rows = queries.shape[0]
    width = key_window.shape[0]
    factor = head_dim ** -0.5
    q_part = queries.reshape(tok_rows, -1, query_per_key_head * head_dim)[:, group].reshape(tok_rows * query_per_key_head, head_dim)
    g_part = grad_out.reshape(tok_rows, -1, query_per_key_head * head_dim)[:, group].reshape(tok_rows * query_per_key_head, head_dim)
    k_part = key_window.reshape(width, -1, head_dim)[:, group]
    v_part = value_window.reshape(width, -1, head_dim)[:, group]
    scores = jnp.dot(q_part, k_part.T, preferred_element_type=jnp.float32) * factor
    mask_rows = jnp.broadcast_to(visible_mask[:, None, :], (tok_rows, query_per_key_head, width)).reshape(tok_rows * query_per_key_head, width)
    top_score = jnp.max(jnp.where(mask_rows, scores, -1e30), axis=1, keepdims=True)
    expo = jnp.where(mask_rows, jnp.exp(scores - top_score), 0.0)
    probs = expo / jnp.sum(expo, axis=1, keepdims=True)
    probs_low = probs.astype(jnp.bfloat16)
    attn_out = jnp.dot(probs_low, v_part, preferred_element_type=jnp.float32)
    delta = jnp.sum(g_part.astype(jnp.float32) * attn_out, axis=1, keepdims=True)
    dprobs = jnp.dot(g_part, v_part.T, preferred_element_type=jnp.float32)
    dscores = (probs * (dprobs - delta)).astype(jnp.bfloat16)
    query_gradient = jnp.dot(dscores, k_part, preferred_element_type=jnp.float32) * factor
    key_gradient = jnp.dot(dscores.T, q_part, preferred_element_type=jnp.float32) * factor
    value_gradient = jnp.dot(probs_low.T, g_part, preferred_element_type=jnp.float32)
    return query_gradient.reshape(tok_rows, query_per_key_head * head_dim), key_gradient, value_gradient


def block_gradient_step(queries, grad_out, key_window, value_window, visible_mask, heads_kv, query_per_key_head, head_dim):
    dq_list, dk_list, dv_list = [], [], []
    for group in range(heads_kv):
        query_gradient, key_gradient, value_gradient = head_group(queries, grad_out, key_window, value_window, visible_mask, group, query_per_key_head, head_dim)
        dq_list.append(query_gradient)
        dk_list.append(key_gradient)
        dv_list.append(value_gradient)
    return jnp.concatenate(dq_list, axis=1), jnp.concatenate(dk_list, axis=1), jnp.concatenate(dv_list, axis=1)


def reference(queries, keys, values, grad_out, doc_start):
    query_per_key_head = QUERY_HEADS // KEY_VALUE_HEADS
    halo_tokens = SPAN * TOK_DEV
    width = (SPAN + 1) * TOK_DEV
    zeroed_rows = jnp.zeros((halo_tokens, KEY_VALUE_HEADS * HEAD_SIZE), jnp.bfloat16)
    key_pad = jnp.concatenate([zeroed_rows, keys], axis=0)
    val_pad = jnp.concatenate([zeroed_rows, values], axis=0)
    empty_accumulator = jnp.zeros((PACKED_TOKENS + halo_tokens, KEY_VALUE_HEADS * HEAD_SIZE), jnp.float32)

    def one_block(carry, block):
        acc_k, acc_v = carry
        first = (block * TOK_DEV).astype(jnp.int32)
        query_block = lax.dynamic_slice_in_dim(queries, first, TOK_DEV, 0)
        output_gradient_block = lax.dynamic_slice_in_dim(grad_out, first, TOK_DEV, 0)
        key_window = lax.dynamic_slice_in_dim(key_pad, first, width, 0)
        value_window = lax.dynamic_slice_in_dim(val_pad, first, width, 0)
        starts = lax.dynamic_slice_in_dim(doc_start, first, TOK_DEV, 0)
        q_pos = first + jnp.arange(TOK_DEV, dtype=jnp.int32)
        k_pos = first - halo_tokens + jnp.arange(width, dtype=jnp.int32)
        visible_mask = (k_pos[None, :] >= starts[:, None]) & (k_pos[None, :] <= q_pos[:, None])
        query_gradient, key_gradient, value_gradient = block_gradient_step(query_block, output_gradient_block, key_window, value_window, visible_mask, KEY_VALUE_HEADS, query_per_key_head, HEAD_SIZE)
        term_k = lax.optimization_barrier(key_gradient.astype(jnp.bfloat16)).astype(jnp.float32)
        term_v = lax.optimization_barrier(value_gradient.astype(jnp.bfloat16)).astype(jnp.float32)
        acc_k = lax.dynamic_update_slice_in_dim(acc_k, lax.dynamic_slice_in_dim(acc_k, first, width, 0) + term_k, first, 0)
        acc_v = lax.dynamic_update_slice_in_dim(acc_v, lax.dynamic_slice_in_dim(acc_v, first, width, 0) + term_v, first, 0)
        return (acc_k, acc_v), query_gradient.astype(jnp.bfloat16)

    blocks = jnp.arange(PACKED_TOKENS // TOK_DEV, dtype=jnp.int32)
    (acc_k, acc_v), dq_blocks = lax.scan(one_block, (empty_accumulator, empty_accumulator), blocks)
    grad_queries = dq_blocks.reshape(PACKED_TOKENS, QUERY_HEADS * HEAD_SIZE)
    grad_keys = acc_k[halo_tokens:].astype(jnp.bfloat16)
    grad_values = acc_v[halo_tokens:].astype(jnp.bfloat16)
    return grad_queries, grad_keys, grad_values
```

```python
import functools

import jax
import jax.numpy as jnp
from jax import lax
from jax.experimental import pallas as pl
from jax.experimental.pallas import tpu as pltpu
from jax.sharding import PartitionSpec as P

HEAD = 128
TOK = 128
SPAN = 4
PER_GROUP = 8
AXES = ("outer", "inner")
F32 = jnp.float32
BF16 = jnp.bfloat16
SCALE = HEAD**-0.5
LOG2E = 1.4426950408889634


def by_parity(x, even, odd):
    peers = lax.axis_size(AXES)
    return lax.ppermute(
        x, AXES, [(i, (i + (odd if i % 2 else even)) % peers) for i in range(peers)]
    )


def with_partner(x):
    peers = lax.axis_size(AXES)
    return lax.ppermute(x, AXES, [(i, i ^ 1) for i in range(peers)])


def rows_by_rows(a, b):
    return lax.dot_general(a, b, (((1,), (1,)), ((), ())), preferred_element_type=F32)


def cols_by_cols(a, b):
    return lax.dot_general(a, b, (((0,), (0,)), ((), ())), preferred_element_type=F32)


def nearest_first(refs, col, odd, count):
    own, both, near, far = refs
    blocks = [own[:, col], both[TOK:, col]]
    if count > 2:
        blocks.append(jnp.where(odd, near[:, col], far[:, col]))
    if count > 3:
        blocks.append(both[:TOK, col])
    if count > 4:
        blocks.append(jnp.where(odd, far[:, col], near[:, col]))
    return jnp.concatenate(blocks, axis=0)


def spread(refs, col, odd, count, x):
    own, both, near, far = refs
    rows = [x[n * TOK : (n + 1) * TOK].astype(BF16) for n in range(count)]
    rows += [jnp.zeros((TOK, HEAD), BF16)] * (SPAN + 1 - count)
    own[:, col] = rows[0]
    both[:, col] = jnp.concatenate([rows[3], rows[1]], axis=0)
    near[:, col] = jnp.where(odd, rows[2], rows[4])
    far[:, col] = jnp.where(odd, rows[4], rows[2])


def heads_stacked(ref):
    return jnp.concatenate([ref[:, h * HEAD : (h + 1) * HEAD] for h in range(PER_GROUP)], axis=0)


def for_each_count(info, attend):
    for count in range(2, SPAN + 2):
        pl.when(info[0] == count)(functools.partial(attend, count))


def probs_kernel(info, starts, q_ref, g_ref, *refs):
    k_refs, p_ref, terms, bias_ref = refs[:4], refs[4], refs[5:9], refs[9]
    i = pl.program_id(0)
    odd = info[1] == 1

    @pl.when(i == 0)
    def _():
        qi = lax.broadcasted_iota(jnp.int32, (TOK, TOK), 1)
        ji = lax.broadcasted_iota(jnp.int32, (TOK, TOK), 0)
        for back in range(SPAN + 1):
            kj = ji - back * TOK
            seen = kj >= starts[...]
            if back == 0:
                seen = seen & (kj <= qi)
            bias_ref[pl.ds(back * TOK, TOK), :] = jnp.where(seen, 0.0, -jnp.inf)

    col = pl.ds(pl.multiple_of(i * HEAD, HEAD), HEAD)

    def attend(count):
        keys = nearest_first(k_refs, col, odd, count)
        bias = jnp.concatenate([bias_ref[: count * TOK, :]] * PER_GROUP, axis=1)
        scores = rows_by_rows(keys, heads_stacked(q_ref)) + bias
        top = jnp.max(scores, axis=0, keepdims=True)
        expo = jnp.exp2((scores - top) * (SCALE * LOG2E))
        low = (expo * (1.0 / jnp.sum(expo, axis=0, keepdims=True))).astype(BF16)
        p_ref[0, : count * TOK, :] = low
        dv = jnp.dot(low, heads_stacked(g_ref), preferred_element_type=F32)
        spread(terms, col, odd, count, dv)

    for_each_count(info, attend)


def scores_kernel(info, q_ref, g_ref, p_ref, *refs):
    k_refs, v_refs, dq_ref, terms = refs[:4], refs[4:8], refs[8], refs[9:13]
    i = pl.program_id(0)
    odd = info[1] == 1
    col = pl.ds(pl.multiple_of(i * HEAD, HEAD), HEAD)

    def attend(count):
        keys = nearest_first(k_refs, col, odd, count)
        vals = nearest_first(v_refs, col, odd, count)
        probs = p_ref[0, : count * TOK, :].astype(F32)
        weighted = probs * rows_by_rows(vals, heads_stacked(g_ref))
        delta = jnp.sum(weighted, axis=0, keepdims=True)
        dscores = (weighted - probs * delta).astype(BF16)
        dk = jnp.dot(dscores, heads_stacked(q_ref), preferred_element_type=F32) * SCALE
        dq = cols_by_cols(keys, dscores) * SCALE
        for h in range(PER_GROUP):
            part = slice(h * HEAD, (h + 1) * HEAD)
            dq_ref[:, part] = dq[:, part].T.astype(BF16)
        spread(terms, col, odd, count, dk)

    for_each_count(info, attend)


def whole(i):
    return (0, 0)


WIDE = pl.BlockSpec((TOK, PER_GROUP * HEAD), lambda i: (0, i))


def call(kernel, name, groups, in_specs, out_specs, out_shape, scratch, *args):
    pairs = TOK * PER_GROUP * TOK * (SPAN + 1) * groups
    return pl.pallas_call(
        kernel,
        grid=(groups,),
        in_specs=in_specs,
        out_specs=out_specs,
        out_shape=out_shape,
        scratch_shapes=scratch,
        compiler_params=pltpu.CompilerParams(vmem_limit_bytes=40 * 2**20),
        cost_estimate=pl.CostEstimate(
            flops=pairs * HEAD * 5, bytes_accessed=2**21, transcendentals=pairs
        ),
        name=name,
    )(*args)


def gathered(own, odd):
    near = by_parity(own, 4, 2)
    far = by_parity(own, 2, 4)
    both = with_partner(jnp.concatenate([far, jnp.where(odd, near, own)], axis=0))
    return [pltpu.with_memory_space_constraint(own, pltpu.HBM), both, near, far]


def returned(own, both, near, far, odd):
    both = with_partner(both).astype(F32)
    far = (far.astype(F32) + both[:TOK]).astype(BF16)
    near = (near.astype(F32) + jnp.where(odd, both[TOK:], 0)).astype(BF16)
    own = own.astype(F32) + jnp.where(odd, 0, both[TOK:])
    far = by_parity(far, -2, -4)
    near = by_parity(near, -4, -2)
    return (own + far.astype(F32) + near.astype(F32)).astype(BF16)


def body(queries, keys, values, grad_out, doc_start):
    groups = keys.shape[1] // HEAD
    queries = pltpu.with_memory_space_constraint(queries, pltpu.HBM)
    grad_out = pltpu.with_memory_space_constraint(grad_out, pltpu.HBM)
    index = lax.axis_index(AXES).astype(jnp.int32)
    odd = index % 2 == 1
    starts = doc_start.reshape(1, TOK) - index * TOK
    reach = (index * TOK - doc_start[0] + TOK - 1) // TOK
    info = jnp.stack([jnp.clip(reach + 1, 2, SPAN + 1), index % 2])
    k_window = gathered(keys, odd)
    v_window = gathered(values, odd)
    blocks = [pl.BlockSpec(x.shape, whole) for x in k_window]
    terms = [jax.ShapeDtypeStruct(x.shape, BF16) for x in k_window]
    width = (SPAN + 1) * TOK
    p_shape = (groups, width, PER_GROUP * TOK)
    p_spec = pl.BlockSpec((1,) + p_shape[1:], lambda i: (i, 0, 0))
    probs, *v_terms = call(
        probs_kernel,
        "probs",
        groups,
        [pl.BlockSpec(memory_space=pltpu.SMEM), pl.BlockSpec((1, TOK), whole), WIDE, WIDE] + blocks,
        [p_spec] + blocks,
        [jax.ShapeDtypeStruct(p_shape, BF16)] + terms,
        [pltpu.VMEM((width, TOK), F32)],
        info,
        starts,
        queries,
        grad_out,
        *k_window,
    )
    grad_queries, *k_terms = call(
        scores_kernel,
        "dscores",
        groups,
        [pl.BlockSpec(memory_space=pltpu.SMEM), WIDE, WIDE, p_spec] + blocks * 2,
        [WIDE] + blocks,
        [jax.ShapeDtypeStruct(queries.shape, BF16)] + terms,
        [],
        info,
        queries,
        grad_out,
        probs,
        *k_window,
        *v_window,
    )
    grad_values = returned(*v_terms, odd)
    grad_keys = returned(*k_terms, odd)
    return grad_queries, grad_keys, grad_values


def solution(mesh):
    rows = P(AXES, None)
    return jax.shard_map(
        body,
        mesh=mesh,
        in_specs=(rows, rows, rows, rows, P(AXES)),
        out_specs=(rows, rows, rows),
        check_vma=False,
    )
```

```python
import functools

import jax
import jax.numpy as jnp
from jax import lax
from jax.experimental import pallas as pl
from jax.experimental.pallas import tpu as pltpu
from jax.sharding import PartitionSpec as P

HEAD = 128
TOK = 128
SPAN = 4
PER_GROUP = 8
AXES = ("outer", "inner")
F32 = jnp.float32
BF16 = jnp.bfloat16
SCALE = HEAD**-0.5
LOG2E = 1.4426950408889634


def by_parity(x, even, odd):
    peers = lax.axis_size(AXES)
    return lax.ppermute(
        x, AXES, [(i, (i + (odd if i % 2 else even)) % peers) for i in range(peers)]
    )


def with_partner(x):
    peers = lax.axis_size(AXES)
    return lax.ppermute(x, AXES, [(i, i ^ 1) for i in range(peers)])


def rows_by_rows(a, b):
    return lax.dot_general(a, b, (((1,), (1,)), ((), ())), preferred_element_type=F32)


def cols_by_cols(a, b):
    return lax.dot_general(a, b, (((0,), (0,)), ((), ())), preferred_element_type=F32)


def nearest_first(refs, col, odd, count):
    own, both, near, far = refs
    blocks = [own[:, col], both[TOK:, col]]
    if count > 2:
        blocks.append(jnp.where(odd, near[:, col], far[:, col]))
    if count > 3:
        blocks.append(both[:TOK, col])
    if count > 4:
        blocks.append(jnp.where(odd, far[:, col], near[:, col]))
    return jnp.concatenate(blocks, axis=0)


def spread(refs, col, odd, count, x):
    own, both, near, far = refs
    rows = [x[n * TOK : (n + 1) * TOK].astype(BF16) for n in range(count)]
    rows += [jnp.zeros((TOK, HEAD), BF16)] * (SPAN + 1 - count)
    own[:, col] = rows[0]
    both[:, col] = jnp.concatenate([rows[3], rows[1]], axis=0)
    near[:, col] = jnp.where(odd, rows[2], rows[4])
    far[:, col] = jnp.where(odd, rows[4], rows[2])


def heads_stacked(ref):
    return jnp.concatenate([ref[:, h * HEAD : (h + 1) * HEAD] for h in range(PER_GROUP)], axis=0)


def for_each_count(info, attend):
    for count in range(2, SPAN + 2):
        pl.when(info[0] == count)(functools.partial(attend, count))


def probs_kernel(info, starts, q_ref, g_ref, *refs):
    k_refs, p_ref, terms, bias_ref = refs[:4], refs[4], refs[5:9], refs[9]
    i = pl.program_id(0)
    odd = info[1] == 1

    @pl.when(i == 0)
    def _():
        qi = lax.broadcasted_iota(jnp.int32, (TOK, TOK), 1)
        ji = lax.broadcasted_iota(jnp.int32, (TOK, TOK), 0)
        for back in range(SPAN + 1):
            kj = ji - back * TOK
            seen = kj >= starts[...]
            if back == 0:
                seen = seen & (kj <= qi)
            bias_ref[pl.ds(back * TOK, TOK), :] = jnp.where(seen, 0.0, -jnp.inf)

    col = pl.ds(pl.multiple_of(i * HEAD, HEAD), HEAD)

    def attend(count):
        keys = nearest_first(k_refs, col, odd, count)
        bias = jnp.concatenate([bias_ref[: count * TOK, :]] * PER_GROUP, axis=1)
        scores = rows_by_rows(keys, heads_stacked(q_ref)) + bias
        top = jnp.max(scores, axis=0, keepdims=True)
        expo = jnp.exp2((scores - top) * (SCALE * LOG2E))
        low = (expo * (1.0 / jnp.sum(expo, axis=0, keepdims=True))).astype(BF16)
        p_ref[0, : count * TOK, :] = low
        dv = jnp.dot(low, heads_stacked(g_ref), preferred_element_type=F32)
        spread(terms, col, odd, count, dv)

    for_each_count(info, attend)


def scores_kernel(info, q_ref, g_ref, p_ref, *refs):
    k_refs, v_refs, dq_ref, terms = refs[:4], refs[4:8], refs[8], refs[9:13]
    i = pl.program_id(0)
    odd = info[1] == 1
    col = pl.ds(pl.multiple_of(i * HEAD, HEAD), HEAD)

    def attend(count):
        keys = nearest_first(k_refs, col, odd, count)
        vals = nearest_first(v_refs, col, odd, count)
        probs = p_ref[0, : count * TOK, :].astype(F32)
        weighted = probs * rows_by_rows(vals, heads_stacked(g_ref))
        delta = jnp.sum(weighted, axis=0, keepdims=True)
        dscores = (weighted - probs * delta).astype(BF16)
        dk = jnp.dot(dscores, heads_stacked(q_ref), preferred_element_type=F32) * SCALE
        dq = cols_by_cols(keys, dscores) * SCALE
        for h in range(PER_GROUP):
            part = slice(h * HEAD, (h + 1) * HEAD)
            dq_ref[:, part] = dq[:, part].T.astype(BF16)
        spread(terms, col, odd, count, dk)

    for_each_count(info, attend)


def whole(i):
    return (0, 0)


WIDE = pl.BlockSpec((TOK, PER_GROUP * HEAD), lambda i: (0, i))


def call(kernel, name, groups, in_specs, out_specs, out_shape, scratch, *args):
    pairs = TOK * PER_GROUP * TOK * (SPAN + 1) * groups
    return pl.pallas_call(
        kernel,
        grid=(groups,),
        in_specs=in_specs,
        out_specs=out_specs,
        out_shape=out_shape,
        scratch_shapes=scratch,
        compiler_params=pltpu.CompilerParams(vmem_limit_bytes=40 * 2**20),
        cost_estimate=pl.CostEstimate(
            flops=pairs * HEAD * 5, bytes_accessed=2**21, transcendentals=pairs
        ),
        name=name,
    )(*args)


def gathered(own, odd):
    near = by_parity(own, 4, 2)
    far = by_parity(own, 2, 4)
    both = with_partner(jnp.concatenate([far, jnp.where(odd, near, own)], axis=0))
    return [own, both, near, far]


def returned(own, both, near, far, odd):
    both = with_partner(both).astype(F32)
    far = (far.astype(F32) + both[:TOK]).astype(BF16)
    near = (near.astype(F32) + jnp.where(odd, both[TOK:], 0)).astype(BF16)
    own = own.astype(F32) + jnp.where(odd, 0, both[TOK:])
    far = by_parity(far, -2, -4)
    near = by_parity(near, -4, -2)
    return (own + far.astype(F32) + near.astype(F32)).astype(BF16)


def body(queries, keys, values, grad_out, doc_start):
    groups = keys.shape[1] // HEAD
    index = lax.axis_index(AXES).astype(jnp.int32)
    odd = index % 2 == 1
    starts = doc_start.reshape(1, TOK) - index * TOK
    reach = (index * TOK - doc_start[0] + TOK - 1) // TOK
    info = jnp.stack([jnp.clip(reach + 1, 2, SPAN + 1), index % 2])
    k_window = gathered(keys, odd)
    v_window = gathered(values, odd)
    blocks = [pl.BlockSpec(x.shape, whole) for x in k_window]
    terms = [jax.ShapeDtypeStruct(x.shape, BF16) for x in k_window]
    width = (SPAN + 1) * TOK
    p_shape = (groups, width, PER_GROUP * TOK)
    p_spec = pl.BlockSpec((1,) + p_shape[1:], lambda i: (i, 0, 0))
    probs, *v_terms = call(
        probs_kernel,
        "probs",
        groups,
        [pl.BlockSpec(memory_space=pltpu.SMEM), pl.BlockSpec((1, TOK), whole), WIDE, WIDE] + blocks,
        [p_spec] + blocks,
        [jax.ShapeDtypeStruct(p_shape, BF16)] + terms,
        [pltpu.VMEM((width, TOK), F32)],
        info,
        starts,
        pltpu.with_memory_space_constraint(queries, pltpu.HBM),
        pltpu.with_memory_space_constraint(grad_out, pltpu.HBM),
        pltpu.with_memory_space_constraint(k_window[0], pltpu.HBM),
        *k_window[1:],
    )
    grad_queries, *k_terms = call(
        scores_kernel,
        "dscores",
        groups,
        [pl.BlockSpec(memory_space=pltpu.SMEM), WIDE, WIDE, p_spec] + blocks * 2,
        [WIDE] + blocks,
        [jax.ShapeDtypeStruct(queries.shape, BF16)] + terms,
        [],
        info,
        queries,
        grad_out,
        probs,
        *k_window,
        *v_window,
    )
    grad_values = returned(*v_terms, odd)
    grad_keys = returned(*k_terms, odd)
    return grad_queries, grad_keys, grad_values


def solution(mesh):
    rows = P(AXES, None)
    return jax.shard_map(
        body,
        mesh=mesh,
        in_specs=(rows, rows, rows, rows, P(AXES)),
        out_specs=(rows, rows, rows),
        check_vma=False,
    )
```
